32 devices in a mesh: dp: 4 (over z), expert: 8 (over y, x, core).
Axes of the slice: x: 2, y: 2, z: 4, core: 2. Of those that a mesh axis runs over, the one named last changes fastest.
Arguments:
- tokens: bfloat16 [1024, 7168], P('expert', 'dp'), may hold values from -6 to 6
- routes: int32 [1024, 4], P('expert'), may hold values from 0 to 7, all different within a row; in each aligned block of 128 rows (0 to 127, 128 to 255, ...) at most 96 rows name the same one
- gate_probs: float32 [1024, 4], P('expert'), may hold values from 0.05 to 0.5
- gate_up_weight: bfloat16 [8, 7168, 2, 1024], P('expert', 'dp'), may hold values from -0.0625 to 0.0625
- down_weight: bfloat16 [8, 1024, 7168], P('expert', None, 'dp'), may hold values from -0.1875 to 0.1875
- cotangent: bfloat16 [1024, 7168], P('expert', 'dp'), may hold values from -6 to 6
Outputs:
- mixed: bfloat16 [1024, 7168], P('expert', 'dp')
- token_grad: bfloat16 [1024, 7168], P('expert', 'dp')
- prob_grad: float32 [1024, 4], P('expert')
- gate_up_grad: bfloat16 [8, 7168, 2, 1024], P('expert', 'dp')
- down_grad: bfloat16 [8, 1024, 7168], P('expert', None, 'dp')
The draws below stay inside these ranges and needn't reach their ends.
Inputs may be any that keep to these rules, and one draw needn't show every extreme that they name: `routes`: each row names 4 different experts. In each aligned block of 128 rows (the rows of one device) no expert is named by more than 96 rows, a bound that some block reaches.
All inputs are finite; a program needn't handle non-finite values.
Results may differ from the reference program's by a relative error of at most 0.0065.
Values may be sent and summed in bfloat16 or wider, within the bound.
No kernel may reach another device: no remote copies, remote signals or barrier semaphores. Data moves between devices by JAX's collectives and lax.ppermute only.
A program may use at most 128 MiB of HBM per device.

```python
import math
from functools import partial
import jax
import jax.numpy as jnp
import numpy as np
from jax import lax

D = 7168
FF = 1024
TOPK = 4
TOK_DEV = 128
EXPERTS = 8
CAP = 96
TOKENS = 1024


def levels(rng, dims, cuts, least, high):
    def one(axis_at, blocks):
        draws = jax.random.uniform(jax.random.fold_in(jax.random.fold_in(rng, 6), axis_at), (blocks,), jnp.float32, least / len(cuts), high / len(cuts))
        return jnp.repeat(jnp.exp(draws), dims[axis_at] // blocks).reshape((-1,) + (1,) * (len(dims) - axis_at - 1))

    factor_of = one(*cuts[0])
    for cut in cuts[1:]:
        factor_of = factor_of * one(*cut)
    return factor_of


def deal_out(rng, own, number, rows, count, top, most, skew):
    order = jax.random.permutation(rng, count)
    packed, usual = load_shares(count, rows * top, most, skew, True), load_shares(count, rows * top, most, skew, False)
    places = jnp.arange(count)

    def named(lengths, turn):
        used = int((lengths > 0).sum())
        fixed = max(1, used // 4)
        passed = fixed + (places - fixed + turn * (used - fixed)) % max(1, count - fixed)
        return jnp.zeros((count,), jnp.int32).at[order[jnp.where(places < fixed, places, passed)]].set(jnp.asarray(lengths, jnp.int32))

    lengths = jnp.where(number % 4 == 0, named(packed, number // 4), named(usual, number - number // 4 - 1))
    mixed = jax.random.permutation(jax.random.fold_in(own, 3), count)
    donor, taker = mixed[0:count // 2 * 2:2], mixed[1:count // 2 * 2:2]
    margin = jnp.minimum(lengths[donor] - 1, most - lengths[taker]) // 2
    margin = jnp.where((donor == order[0]) | (taker == order[0]) | (lengths[taker] == 0), 0, jnp.maximum(margin, 0))
    passed = jax.random.randint(jax.random.fold_in(own, 4), (count // 2,), 0, 1 << 20) % (margin + 1)
    lengths = lengths.at[donor].add(-passed).at[taker].add(passed)
    labels = jnp.searchsorted(jnp.cumsum(lengths), jnp.arange(rows * top), side="right").astype(jnp.int32)
    table = labels.reshape(top, rows).T
    table = table[jax.random.permutation(jax.random.fold_in(own, 1), rows)]
    turn = jax.random.randint(jax.random.fold_in(own, 2), (rows, 1), 0, top)
    return jnp.take_along_axis(table, (jnp.arange(top)[None, :] + turn) % top, axis=1)


def load_shares(amount, total, most, skew, full):
    weights = [(1 << 20) // math.isqrt(grade ** skew) + 1 for grade in range(1, amount + 1)]
    largest = most if full else min(most, max(-(-total // amount), total * weights[0] // sum(weights)))
    least = 1 if total - largest >= amount - 1 else 0
    counts, spare = [largest] + [least] * (amount - 1), total - largest - least * (amount - 1)
    while spare > 0:
        candidates = [i for i in range(1, amount) if counts[i] < largest] or [i for i in range(1, amount) if counts[i] < most]
        pool, remaining = sum([weights[i] for i in candidates]), spare
        for i in candidates:
            more = min(most - counts[i], max(1, remaining * weights[i] // pool), spare)
            counts[i] = counts[i] + more
            spare = spare - more
    return np.array(counts)


def gaussian(rng, dims, width, limit, cuts=(), kind=jnp.bfloat16):
    entries = jax.random.normal(rng, dims, jnp.float32) * width
    if len(cuts) > 0:
        entries = levels(rng, dims, cuts, -0.22, 0.18) * entries
    return jnp.clip(entries, min=-limit, max=limit).astype(kind)


def setup_inputs(seed: int = 0) -> dict:
    streams_of = jax.random.split(jax.random.key(seed), 7)
    tokens = gaussian(streams_of[0], (TOKENS, D), 1.0, 6.0, ((0, 8), (1, 4)))
    routes_keys = jax.random.split(jax.random.fold_in(streams_of[1], 1), TOKENS // TOK_DEV)
    routes_turns = jax.random.permutation(jax.random.fold_in(streams_of[1], 3), TOKENS // TOK_DEV)
    routes = jax.vmap(lambda own, number: deal_out(jax.random.fold_in(streams_of[1], 2), own, number, TOK_DEV, EXPERTS, TOPK, CAP, 2))(routes_keys, routes_turns).reshape((TOKENS, TOPK))
    gate_probs = jnp.clip(jnp.exp(math.log(0.5) - 2.3025851 * jax.random.uniform(streams_of[2], (TOKENS, TOPK), jnp.float32) ** levels(streams_of[2], (TOKENS, TOPK), ((0, 8),), -0.2, 0.2)), 0.05, 0.5)
    gate_up_weight = gaussian(streams_of[3], (EXPERTS, D, 2, FF), D ** -0.5, 0.0625, ((0, 8), (1, 4)))
    down_weight = gaussian(streams_of[4], (EXPERTS, FF, D), FF ** -0.5, 0.1875, ((0, 8), (2, 4)))
    cotangent = gaussian(streams_of[5], (TOKENS, D), 1.0, 6.0, ((0, 8), (1, 4)))
    return dict(tokens=tokens, routes=routes, gate_probs=gate_probs, gate_up_weight=gate_up_weight, down_weight=down_weight, cotangent=cotangent)


def silu_parts(pre_act):
    sigmoid_v = jax.nn.sigmoid(pre_act)
    return pre_act * sigmoid_v, sigmoid_v * (1.0 + pre_act * (1.0 - sigmoid_v))


def slot_table(route_block, experts, capacity):
    flat_routes = route_block.reshape(-1)
    onehot = (flat_routes[:, None] == jnp.arange(experts, dtype=jnp.int32)[None, :]).astype(jnp.int32)
    before = jnp.cumsum(onehot, axis=0) - onehot
    position = jnp.sum(before * onehot, axis=1)
    return (flat_routes * capacity + position).astype(jnp.int32)


def expert_pass(gate_up_w, down_w, token_rows, grad_rows):
    model_dim = token_rows.shape[1]
    hidden = down_w.shape[0]
    joined = gate_up_w.reshape(model_dim, 2 * hidden)
    pre_act = jnp.dot(token_rows, joined, preferred_element_type=jnp.float32)
    gate_part = pre_act[:, :hidden]
    up_part = pre_act[:, hidden:]
    activated, slopes = silu_parts(gate_part)
    hidden_act = (activated * up_part).astype(jnp.bfloat16)
    expert_out = jnp.dot(hidden_act, down_w, preferred_element_type=jnp.float32).astype(jnp.bfloat16)
    down_grad = jnp.dot(hidden_act.T, grad_rows, preferred_element_type=jnp.float32).astype(jnp.bfloat16)
    hidden_grad = jnp.dot(grad_rows, down_w.T, preferred_element_type=jnp.float32)
    act_grad = jnp.concatenate([hidden_grad * up_part * slopes, hidden_grad * activated], axis=1).astype(jnp.bfloat16)
    gate_up_grad = jnp.dot(token_rows.T, act_grad, preferred_element_type=jnp.float32).astype(jnp.bfloat16)
    slot_grad = jnp.dot(act_grad, joined.T, preferred_element_type=jnp.float32).astype(jnp.bfloat16)
    return expert_out, slot_grad, gate_up_grad.reshape(model_dim, 2, hidden), down_grad


def reference(tokens, routes, gate_probs, gate_up_weight, down_weight, cotangent):
    tok_total, model_dim = tokens.shape
    blocks = tok_total // TOK_DEV
    per_expert = blocks * CAP
    local_slot = jax.vmap(partial(slot_table, experts=EXPERTS, capacity=CAP))(routes.reshape(blocks, TOK_DEV, TOPK))
    expert_id = local_slot // CAP
    position = local_slot % CAP
    block_ids = jnp.arange(blocks, dtype=jnp.int32)[:, None]
    global_slot = (expert_id * per_expert + block_ids * CAP + position).reshape(-1).astype(jnp.int32)
    token_ids = jnp.repeat(jnp.arange(tok_total, dtype=jnp.int32), TOPK)
    slot_token = jnp.full((EXPERTS * per_expert,), tok_total, jnp.int32).at[global_slot].set(token_ids)
    slot_prob = jnp.zeros((EXPERTS * per_expert,), jnp.float32).at[global_slot].set(gate_probs.reshape(-1).astype(jnp.float32))
    padded_tok = jnp.concatenate([tokens, jnp.zeros((1, model_dim), tokens.dtype)], axis=0)
    padded_cot = jnp.concatenate([cotangent, jnp.zeros((1, model_dim), cotangent.dtype)], axis=0)

    def per_expert_fn(operands):
        gate_up_w, down_w, slot_ids, slot_weight = operands
        token_rows = padded_tok[slot_ids]
        grad_rows = (padded_cot[slot_ids].astype(jnp.float32) * slot_weight[:, None]).astype(jnp.bfloat16)
        return expert_pass(gate_up_w, down_w, token_rows, grad_rows)

    expert_out, slot_grad, gate_up_grad, down_grad = lax.map(
        per_expert_fn,
        (gate_up_weight, down_weight, slot_token.reshape(EXPERTS, per_expert), slot_prob.reshape(EXPERTS, per_expert)))
    returned = expert_out.reshape(-1, model_dim)[global_slot].reshape(tok_total, TOPK, model_dim).astype(jnp.float32)
    returned_grad = slot_grad.reshape(-1, model_dim)[global_slot].reshape(tok_total, TOPK, model_dim).astype(jnp.float32)
    probs_wide = gate_probs.astype(jnp.float32)
    mixed = jnp.sum(probs_wide[:, :, None] * returned, axis=1).astype(jnp.bfloat16)
    prob_grad = jnp.sum(returned * cotangent.astype(jnp.float32)[:, None, :], axis=2)
    token_grad = jnp.sum(returned_grad, axis=1).astype(jnp.bfloat16)
    return (mixed, token_grad, prob_grad, gate_up_grad, down_grad)
```

```python
import jax
import jax.numpy as jnp
from jax import lax
from jax.experimental import pallas as pl
from jax.experimental.pallas import tpu as pltpu
from jax.sharding import PartitionSpec as P

BF16 = jnp.bfloat16
F32 = jnp.float32
LANES = 128
HALVES = 8


def exact_parts(values):
    first = lax.reduce_precision(values, 8, 7)
    rest = values - first
    second = lax.reduce_precision(rest, 8, 7)
    third = rest - second
    return [first, second, third]


def nothing(*refs):
    pass


def after(array, *results):
    return pl.pallas_call(
        nothing,
        out_shape=jax.ShapeDtypeStruct(array.shape, array.dtype),
        in_specs=[pl.BlockSpec(memory_space=pl.ANY)] * (1 + len(results)),
        out_specs=pl.BlockSpec(memory_space=pl.ANY),
        input_output_aliases={0: 0},
        compiler_params=pltpu.CompilerParams(vmem_limit_bytes=1 << 17),
        name="after",
    )(array, *results)


def swap(array, bit):
    size = lax.axis_size("expert")
    return lax.ppermute(array, "expert", [(i, i ^ bit) for i in range(size)])


def with_other_core(part):
    return jnp.concatenate([part, swap(part, 1)], axis=0)


def line_pipeline(partial_of, owned, order, at_end, back):
    count = len(order)
    last = lax.axis_size("dp") - 1
    outer = [(0, 1), (1, 0), (last, last - 1), (last - 1, last)]
    middle = [(1, 2), (2, 1)]
    near, far = [], []
    from_outer, from_middle, own = {}, {}, {}
    result = {}
    for step in range(2 * count + 2):
        inward = outward = between = None
        if step < count:
            near_half, inward, far_half = partial_of(step, from_outer.get(step - 1))
            near.append(near_half)
            far.append(far_half)
        elif step < 2 * count:
            inward = own[order[step - count]]
        if 2 <= step < count + 2:
            g = step - 2
            outward = (near[g] + from_middle[step - 1].astype(F32)).astype(BF16)
        elif step >= count + 2:
            outward = from_middle[step - 1]
            if step >= count + 4:
                outward = after(outward, back(order[step - count - 4], result[order[step - count - 4]]))
        if inward is None or outward is None:
            operand = outward if inward is None else inward
        else:
            outward = jnp.pad(outward, ((0, 0), (0, inward.shape[1] - outward.shape[1])))
            operand = jnp.where(at_end, inward, outward)
        if 1 <= step <= count:
            between = (far[step - 1] + from_outer[step - 1].astype(F32)).astype(BF16)
        elif count < step <= 2 * count:
            between = from_outer[step - 1]
        from_outer[step] = lax.ppermute(operand, "dp", outer)
        if between is not None:
            from_middle[step] = lax.ppermute(between, "dp", middle)
        if 2 <= step < count + 2:
            own[step - 2] = owned(step - 2, near[step - 2] + from_outer[step][:, : near[step - 2].shape[1]].astype(F32))
        elif step >= count + 2:
            g = order[step - count - 2]
            result[g] = (
                jnp.where(at_end, own[g], from_outer[step - 2]),
                jnp.where(at_end, from_outer[step], from_middle[step - 1]),
            )
    return result


def shards(tokens, routes, gate_probs, gate_up_weight, down_weight, cotangent):
    tok_rows, model_part = tokens.shape
    top_count = routes.shape[1]
    hidden = down_weight.shape[1]
    experts = lax.axis_size("expert")
    capacity = 3 * tok_rows * top_count // (2 * experts)
    half_blocks = experts // HALVES
    half_rows = half_blocks * capacity
    group_tokens = 2 * half_blocks * tok_rows
    group_rows = 2 * half_rows
    mine = lax.axis_index("expert")
    place = lax.axis_index("dp")
    side = (place >= 2).astype(jnp.int32)
    at_end = (place == 0) | (place == lax.axis_size("dp") - 1)

    weight = gate_up_weight.reshape(model_part, 2 * hidden)
    down = down_weight.reshape(hidden, model_part)

    info = jnp.concatenate([routes.astype(F32)] + exact_parts(gate_probs), axis=1)
    info = jnp.pad(info, ((0, 0), (0, LANES - info.shape[1]))).astype(BF16)
    block = jnp.concatenate([tokens, cotangent, info], axis=1)
    near_first = experts == 8
    if near_first:
        blocks = [block, swap(block, 2), swap(block, 4), None]
    else:
        whole = lax.all_gather(block, "expert", axis=0, tiled=True)
        blocks = jnp.split(whole, 4, axis=0)

    lane = lax.broadcasted_iota(jnp.int32, (tok_rows, tok_rows), 1)
    row = lax.broadcasted_iota(jnp.int32, (tok_rows, tok_rows), 0)
    earlier = (lane < row).astype(BF16)
    group_block = jnp.arange(2 * half_blocks, dtype=jnp.int32)
    first_row = ((group_block // half_blocks) ^ side) * half_rows + (group_block % half_blocks) * capacity
    mine_f = mine.astype(F32)

    def front(group):
        named = group[:, 2 * model_part : 2 * model_part + top_count].astype(F32) == mine_f
        named = jnp.any(named, axis=1).reshape(2 * half_blocks, tok_rows)
        before = jnp.dot(named.astype(BF16), earlier.T, preferred_element_type=F32).astype(jnp.int32)
        target = jnp.where(named, before + first_row[:, None], -1).reshape(group_tokens, 1)
        pick = (target == lax.broadcasted_iota(jnp.int32, (group_tokens, group_rows), 1)).astype(BF16)
        picked = lax.dot_general(pick, group, (((0,), (0,)), ((), ())), preferred_element_type=F32).astype(BF16)
        token_rows = picked[:, :model_part]
        grad_rows = picked[:, model_part : 2 * model_part]
        slot_info = picked[:, 2 * model_part :].astype(F32)
        prob = sum(
            slot_info[:, top_count * i : top_count * (i + 1)] for i in (1, 2, 3)
        )
        prob = jnp.sum(jnp.where(slot_info[:, :top_count] == mine_f, prob, 0.0), axis=1, keepdims=True)
        pre = jnp.dot(token_rows, weight, preferred_element_type=F32)
        hidden_grad = lax.dot_general(grad_rows, down, (((1,), (1,)), ((), ())), preferred_element_type=F32)
        partial = jnp.concatenate([pre, hidden_grad], axis=1)
        far = partial[half_rows:].astype(BF16)
        return pick, token_rows, grad_rows, prob, (partial[:half_rows], far, partial[half_rows:]), far

    fronts = []

    def partial_of(g, earlier_result):
        part = blocks[g]
        if near_first:
            if g == 1:
                part = after(part, earlier_result)
            elif g >= 2:
                part = after(part, fronts[g - 1][5])
            part = with_other_core(part)
        fronts.append(front(part))
        if near_first and g == 0:
            blocks[3] = swap(after(block, fronts[0][5]), 6)
        return fronts[g][4]

    def owned(g, total):
        prob = fronts[g][3][:half_rows]
        gate, up, grad = jnp.split(total, 3, axis=1)
        sigmoid_v = jax.nn.sigmoid(gate)
        activated = gate * sigmoid_v
        slopes = sigmoid_v * (1.0 + gate * (1.0 - sigmoid_v))
        act = activated * up
        lanes = lax.broadcasted_iota(jnp.int32, (half_rows, LANES), 1)
        terms = exact_parts(jnp.sum(act * grad, axis=1, keepdims=True))
        extra = sum(jnp.where(lanes == i * experts + mine, terms[i], 0.0) for i in range(3))
        grad = grad * prob
        return jnp.concatenate([act * prob, grad * up * slopes, grad * activated, extra], axis=1).astype(BF16)

    full, wide, sent = {}, {}, {}
    part_rows = group_tokens // 2

    def back(g, halves):
        full[g] = jnp.concatenate(halves, axis=0)
        out = jnp.dot(full[g][:, :hidden], down, preferred_element_type=F32).astype(BF16)
        slot_grad = lax.dot_general(
            full[g][:, hidden : 3 * hidden], weight, (((1,), (1,)), ((), ())), preferred_element_type=F32
        ).astype(BF16)
        row = jnp.concatenate([out, slot_grad, full[g][:, 3 * hidden :]], axis=1)
        wide[g] = jnp.dot(fronts[g][0], row, preferred_element_type=F32).astype(BF16)
        if not near_first:
            return wide[g]
        other = swap(wide[g][part_rows:], 1)
        sent[g] = wide[g][:part_rows].astype(F32) + other.astype(F32)
        if g:
            sent[g] = swap(sent[g].astype(BF16), 2 * g)
        return other

    order = (1, 2, 3, 0)
    spread = line_pipeline(partial_of, owned, order, at_end, back)
    other = back(3, spread[3])
    back(0, tuple(after(half, other) for half in spread[0]))
    if near_first:
        summed = sum(sent[g].astype(F32) for g in range(4))
    else:
        whole = jnp.concatenate([wide[g] for g in range(4)], axis=0)
        summed = lax.psum_scatter(whole, "expert", scatter_dimension=0, tiled=True).astype(F32)
    mixed = summed[:, :model_part].astype(BF16)
    token_grad = summed[:, model_part : 2 * model_part].astype(BF16)
    extra = summed[:, 2 * model_part :]
    by_expert = sum(extra[:, i * experts : (i + 1) * experts] for i in range(3))
    chosen = routes[:, :, None] == jnp.arange(experts, dtype=jnp.int32)[None, None, :]
    prob_grad = jnp.sum(jnp.where(chosen, by_expert[:, None, :], 0.0), axis=2)

    token_rows = jnp.concatenate([f[1] for f in fronts], axis=0)
    grad_rows = jnp.concatenate([f[2] for f in fronts], axis=0)
    all_rows = jnp.concatenate([full[g] for g in range(4)], axis=0)
    across = (((0,), (0,)), ((), ()))
    down_grad = lax.dot_general(
        all_rows[:, :hidden], grad_rows, across, preferred_element_type=F32
    ).astype(BF16)
    gate_up_grad = lax.dot_general(
        token_rows, all_rows[:, hidden : 3 * hidden], across, preferred_element_type=F32
    ).astype(BF16)
    return (
        mixed,
        token_grad,
        prob_grad,
        gate_up_grad.reshape(1, model_part, 2, hidden),
        down_grad.reshape(1, hidden, model_part),
    )


def solution(mesh):
    placed = (
        P("expert", "dp"),
        P("expert", None),
        P("expert", None),
        P("expert", "dp", None, None),
        P("expert", None, "dp"),
        P("expert", "dp"),
    )
    return jax.shard_map(
        shards,
        mesh=mesh,
        in_specs=placed,
        out_specs=(
            P("expert", "dp"),
            P("expert", "dp"),
            P("expert", None),
            P("expert", "dp", None, None),
            P("expert", None, "dp"),
        ),
        check_vma=False,
    )
```

```python
import functools

import jax
import jax.numpy as jnp
from jax import lax
from jax.experimental import pallas as pl
from jax.experimental.pallas import tpu as pltpu
from jax.sharding import PartitionSpec as P

BF16 = jnp.bfloat16
F32 = jnp.float32
LANES = 128
BLOCK = 256
HALVES = 8


def exact_parts(values):
    first = lax.reduce_precision(values, 8, 7)
    rest = values - first
    second = lax.reduce_precision(rest, 8, 7)
    third = rest - second
    return [first, second, third]


def nothing(*refs):
    pass


def after(array, *results):
    return pl.pallas_call(
        nothing,
        out_shape=jax.ShapeDtypeStruct(array.shape, array.dtype),
        in_specs=[pl.BlockSpec(memory_space=pl.ANY)] * (1 + len(results)),
        out_specs=pl.BlockSpec(memory_space=pl.ANY),
        input_output_aliases={0: 0},
        compiler_params=pltpu.CompilerParams(vmem_limit_bytes=1 << 17),
        name="after",
    )(array, *results)


def grad_block(columns, left_ref, right_ref, out_ref):
    left = left_ref[...]
    out_ref[...] = lax.dot_general(
        left, right_ref[:, columns], (((0,), (0,)), ((), ())), preferred_element_type=F32
    ).astype(BF16)


def weight_grad(left, left_cols, right, right_cols):
    rows = left.shape[0]
    first = left_cols[0] // BLOCK
    wide = right_cols[1]
    return pl.pallas_call(
        functools.partial(grad_block, slice(right_cols[0], right_cols[0] + wide)),
        grid=(left_cols[1] // BLOCK,),
        out_shape=jax.ShapeDtypeStruct((left_cols[1], wide), BF16),
        in_specs=[
            pl.BlockSpec((rows, BLOCK), lambda i: (0, first + i)),
            pl.BlockSpec(right.shape, lambda i: (0, 0)),
        ],
        out_specs=pl.BlockSpec((BLOCK, wide), lambda i: (i, 0)),
        compiler_params=pltpu.CompilerParams(vmem_limit_bytes=24 << 20),
        cost_estimate=pl.CostEstimate(flops=0, bytes_accessed=0, transcendentals=0),
        name="weight_grad",
    )(left, right)


def swap(array, bit):
    size = lax.axis_size("expert")
    return lax.ppermute(array, "expert", [(i, i ^ bit) for i in range(size)])


def with_other_core(part):
    return jnp.concatenate([part, swap(part, 1)], axis=0)


def line_pipeline(count, partial_of, owned, at_end, back):
    last = lax.axis_size("dp") - 1
    inward = [(0, 1), (last, last - 1)]
    middle = [(1, 2), (2, 1)]
    outward = [(1, 0), (2, last)]
    items = 2 * count
    partials = [partial_of(0)]
    own = []
    firsts = [lax.ppermute(partials[0][1], "dp", inward)]
    halves = {}
    second, third, middles, between, across, waits, finished = {}, {}, {}, {}, {}, [], []
    for step in range(items + 2):
        if step < items:
            if step + 1 < count:
                partials.append(partial_of(step + 1))
                sent = partials[step + 1][1]
                waits.append(sent)
            elif step + 1 < items:
                sent = own[step + 1 - count]
            arrived = after(firsts[step], *waits)
            if step + 1 < items:
                firsts.append(lax.ppermute(sent, "dp", inward))
            halves[step] = arrived
            if step < count:
                arrived = (partials[step][2] + arrived.astype(F32)).astype(BF16)
            between[step] = arrived
            second[step] = lax.ppermute(arrived, "dp", middle)
        if 1 <= step <= items:
            item = step - 1
            arrived = second[item]
            if step < items:
                arrived = after(arrived, between[step])
            middles[item] = arrived
            if item < count:
                arrived = (partials[item][0] + arrived.astype(F32)).astype(BF16)
            across[item] = arrived
            third[item] = lax.ppermute(arrived, "dp", outward)
        if step >= 2:
            item = step - 2
            arrived = third[item]
            needs = list(finished) if item > count else []
            if item + 1 < items:
                needs.append(across[item + 1])
            if needs:
                arrived = after(arrived, *needs)
            if item < count:
                own.append(owned(item, partials[item][0] + arrived.astype(F32)))
                waits = [own[item]]
            else:
                g = item - count
                near = jnp.where(at_end, own[g], halves[item])
                waits, finished = back(g, near, jnp.where(at_end, arrived, middles[item]))


def shards(tokens, routes, gate_probs, gate_up_weight, down_weight, cotangent):
    tok_rows, model_part = tokens.shape
    top_count = routes.shape[1]
    hidden = down_weight.shape[1]
    experts = lax.axis_size("expert")
    capacity = 3 * tok_rows * top_count // (2 * experts)
    half_blocks = experts // HALVES
    half_rows = half_blocks * capacity
    group_tokens = 2 * half_blocks * tok_rows
    group_rows = 2 * half_rows
    mine = lax.axis_index("expert")
    place = lax.axis_index("dp")
    side = (place >= 2).astype(jnp.int32)
    at_end = (place == 0) | (place == lax.axis_size("dp") - 1)

    weight = gate_up_weight.reshape(model_part, 2 * hidden)
    down = down_weight.reshape(hidden, model_part)

    info = jnp.concatenate([routes.astype(F32)] + exact_parts(gate_probs), axis=1)
    info = jnp.pad(info, ((0, 0), (0, LANES - info.shape[1]))).astype(BF16)
    block = jnp.concatenate([tokens, cotangent, info], axis=1)
    near_first = experts == 8
    if near_first:
        blocks = [block, swap(block, 2), swap(block, 4), None]
    else:
        whole = lax.all_gather(block, "expert", axis=0, tiled=True)
        blocks = jnp.split(whole, 4, axis=0)

    lane = lax.broadcasted_iota(jnp.int32, (tok_rows, tok_rows), 1)
    row = lax.broadcasted_iota(jnp.int32, (tok_rows, tok_rows), 0)
    earlier = (lane < row).astype(BF16)
    group_block = jnp.arange(2 * half_blocks, dtype=jnp.int32)
    first_row = ((group_block // half_blocks) ^ side) * half_rows + (group_block % half_blocks) * capacity
    mine_f = mine.astype(F32)

    def front(group):
        named = group[:, 2 * model_part : 2 * model_part + top_count].astype(F32) == mine_f
        named = jnp.any(named, axis=1).reshape(2 * half_blocks, tok_rows)
        before = jnp.dot(named.astype(BF16), earlier.T, preferred_element_type=F32).astype(jnp.int32)
        target = jnp.where(named, before + first_row[:, None], -1).reshape(group_tokens, 1)
        pick = (target == lax.broadcasted_iota(jnp.int32, (group_tokens, group_rows), 1)).astype(BF16)
        picked = lax.dot_general(pick, group, (((0,), (0,)), ((), ())), preferred_element_type=F32).astype(BF16)
        token_rows = picked[:, :model_part]
        grad_rows = picked[:, model_part : 2 * model_part]
        slot_info = picked[:, 2 * model_part :].astype(F32)
        prob = sum(
            slot_info[:, top_count * i : top_count * (i + 1)] for i in (1, 2, 3)
        )
        prob = jnp.sum(jnp.where(slot_info[:, :top_count] == mine_f, prob, 0.0), axis=1, keepdims=True)
        pre = jnp.dot(token_rows, weight, preferred_element_type=F32)
        hidden_grad = lax.dot_general(grad_rows, down, (((1,), (1,)), ((), ())), preferred_element_type=F32)
        partial = jnp.concatenate([pre, hidden_grad], axis=1)
        far = partial[half_rows:].astype(BF16)
        return pick, token_rows, grad_rows, prob, (partial[:half_rows], far, partial[half_rows:]), far

    fronts = []

    def partial_of(g):
        part = blocks[g]
        if near_first:
            if g:
                part = after(part, fronts[g - 1][5])
            part = with_other_core(part)
        fronts.append(front(part))
        if near_first and g == 0:
            blocks[3] = swap(after(block, fronts[0][5]), 6)
        return fronts[g][4]

    def owned(g, total):
        prob = fronts[g][3][:half_rows]
        gate, up, grad = jnp.split(total, 3, axis=1)
        sigmoid_v = jax.nn.sigmoid(gate)
        activated = gate * sigmoid_v
        slopes = sigmoid_v * (1.0 + gate * (1.0 - sigmoid_v))
        act = activated * up
        lanes = lax.broadcasted_iota(jnp.int32, (half_rows, LANES), 1)
        terms = exact_parts(jnp.sum(act * grad, axis=1, keepdims=True))
        extra = sum(jnp.where(lanes == i * experts + mine, terms[i], 0.0) for i in range(3))
        grad = grad * prob
        return jnp.concatenate([act * prob, grad * up * slopes, grad * activated, extra], axis=1).astype(BF16)

    full, wide, sent = {}, {}, {}
    part_rows = group_tokens // 2

    grads = {}

    def gate_up():
        token_rows = jnp.concatenate([f[1] for f in fronts], axis=0)
        grads["rows"] = jnp.concatenate([full[i] for i in range(4)], axis=0)
        grads["gate_up"] = weight_grad(token_rows, (0, model_part), grads["rows"], (hidden, 2 * hidden))
        return grads["gate_up"]

    def back(g, near, far):
        full[g] = jnp.concatenate([near, far], axis=0)
        out = jnp.dot(full[g][:, :hidden], down, preferred_element_type=F32).astype(BF16)
        slot_grad = lax.dot_general(
            full[g][:, hidden : 3 * hidden], weight, (((1,), (1,)), ((), ())), preferred_element_type=F32
        ).astype(BF16)
        row = jnp.concatenate([out, slot_grad, full[g][:, 3 * hidden :]], axis=1)
        wide[g] = jnp.dot(fronts[g][0], row, preferred_element_type=F32).astype(BF16)
        if near_first:
            other = wide[g][part_rows:]
            if g == 3:
                other = after(other, gate_up(), sent[1], sent[2])
            other = swap(other, 1)
            chip_sum = (wide[g][:part_rows].astype(F32) + other.astype(F32)).astype(BF16)
            sent[g] = swap(chip_sum, 2 * g) if g else chip_sum
            return [wide[g]], [chip_sum]
        return [wide[g]], [wide[g]]

    line_pipeline(4, partial_of, owned, at_end, back)
    if near_first:
        summed = sum(sent[g].astype(F32) for g in range(4))
    else:
        whole = jnp.concatenate([wide[g] for g in range(4)], axis=0)
        summed = lax.psum_scatter(whole, "expert", scatter_dimension=0, tiled=True).astype(F32)
    mixed = summed[:, :model_part].astype(BF16)
    token_grad = summed[:, model_part : 2 * model_part].astype(BF16)
    extra = summed[:, 2 * model_part :]
    by_expert = sum(extra[:, i * experts : (i + 1) * experts] for i in range(3))
    chosen = routes[:, :, None] == jnp.arange(experts, dtype=jnp.int32)[None, None, :]
    prob_grad = jnp.sum(jnp.where(chosen, by_expert[:, None, :], 0.0), axis=2)

    if not near_first:
        gate_up()
    gate_up_grad = grads["gate_up"]
    grad_rows = jnp.concatenate([f[2] for f in fronts], axis=0)
    down_grad = weight_grad(grads["rows"], (0, hidden), grad_rows, (0, model_part))
    tiles = gate_up_grad.reshape(model_part // 8, 8, 2, hidden).transpose(0, 2, 1, 3)
    tiles = lax.optimization_barrier(tiles)
    return (
        mixed,
        token_grad,
        prob_grad,
        tiles.transpose(0, 2, 1, 3).reshape(1, model_part, 2, hidden),
        down_grad.reshape(1, hidden, model_part),
    )


def solution(mesh):
    placed = (
        P("expert", "dp"),
        P("expert", None),
        P("expert", None),
        P("expert", "dp", None, None),
        P("expert", None, "dp"),
        P("expert", "dp"),
    )
    return jax.shard_map(
        shards,
        mesh=mesh,
        in_specs=placed,
        out_specs=(
            P("expert", "dp"),
            P("expert", "dp"),
            P("expert", None),
            P("expert", "dp", None, None),
            P("expert", None, "dp"),
        ),
        check_vma=False,
    )
```

```python
import functools

import jax
import jax.numpy as jnp
from jax import lax
from jax.experimental import pallas as pl
from jax.experimental.pallas import tpu as pltpu
from jax.sharding import PartitionSpec as P

BF16 = jnp.bfloat16
F32 = jnp.float32
LANES = 128
BLOCK = 256
HALVES = 8


def exact_parts(values):
    first = lax.reduce_precision(values, 8, 7)
    rest = values - first
    second = lax.reduce_precision(rest, 8, 7)
    third = rest - second
    return [first, second, third]


def nothing(*refs):
    pass


def after(array, *results):
    return pl.pallas_call(
        nothing,
        out_shape=jax.ShapeDtypeStruct(array.shape, array.dtype),
        in_specs=[pl.BlockSpec(memory_space=pl.ANY)] * (1 + len(results)),
        out_specs=pl.BlockSpec(memory_space=pl.ANY),
        input_output_aliases={0: 0},
        compiler_params=pltpu.CompilerParams(vmem_limit_bytes=1 << 17),
        name="after",
    )(array, *results)


def grad_block(columns, left_ref, right_ref, out_ref):
    left = left_ref[...]
    out_ref[...] = lax.dot_general(
        left, right_ref[:, columns], (((0,), (0,)), ((), ())), preferred_element_type=F32
    ).astype(BF16)


def weight_grad(left, left_cols, right, right_cols):
    rows = left.shape[0]
    first = left_cols[0] // BLOCK
    wide = right_cols[1]
    return pl.pallas_call(
        functools.partial(grad_block, slice(right_cols[0], right_cols[0] + wide)),
        grid=(left_cols[1] // BLOCK,),
        out_shape=jax.ShapeDtypeStruct((left_cols[1], wide), BF16),
        in_specs=[
            pl.BlockSpec((rows, BLOCK), lambda i: (0, first + i)),
            pl.BlockSpec(right.shape, lambda i: (0, 0), pipeline_mode=pl.Buffered(1)),
        ],
        out_specs=pl.BlockSpec((BLOCK, wide), lambda i: (i, 0)),
        compiler_params=pltpu.CompilerParams(vmem_limit_bytes=14 << 20),
        cost_estimate=pl.CostEstimate(flops=0, bytes_accessed=0, transcendentals=0),
        name="weight_grad",
    )(left, right)


def swap(array, bit):
    size = lax.axis_size("expert")
    return lax.ppermute(array, "expert", [(i, i ^ bit) for i in range(size)])


def with_other_core(part):
    return jnp.concatenate([part, swap(part, 1)], axis=0)


def line_pipeline(count, partial_of, owned, at_end, back):
    last = lax.axis_size("dp") - 1
    inward = [(0, 1), (last, last - 1)]
    middle = [(1, 2), (2, 1)]
    outward = [(1, 0), (2, last)]
    items = 2 * count
    partials = [partial_of(0)]
    own = []
    firsts = [lax.ppermute(partials[0][1], "dp", inward)]
    halves = {}
    second, third, middles, between, across, waits, finished = {}, {}, {}, {}, {}, [], []
    for step in range(items + 2):
        if step < items:
            if step + 1 < count:
                partials.append(partial_of(step + 1))
                sent = partials[step + 1][1]
                waits.append(sent)
            elif step + 1 < items:
                sent = own[step + 1 - count]
            arrived = after(firsts[step], *waits)
            if step + 1 < items:
                firsts.append(lax.ppermute(sent, "dp", inward))
            halves[step] = arrived
            if step < count:
                arrived = (partials[step][2] + arrived.astype(F32)).astype(BF16)
            between[step] = arrived
            second[step] = lax.ppermute(arrived, "dp", middle)
        if 1 <= step <= items:
            item = step - 1
            arrived = second[item]
            if step < items:
                arrived = after(arrived, between[step])
            middles[item] = arrived
            if item < count:
                arrived = (partials[item][0] + arrived.astype(F32)).astype(BF16)
            across[item] = arrived
            third[item] = lax.ppermute(arrived, "dp", outward)
        if step >= 2:
            item = step - 2
            arrived = third[item]
            needs = list(finished) if item > count else []
            if item + 1 < items:
                needs.append(across[item + 1])
            if needs:
                arrived = after(arrived, *needs)
            if item < count:
                own.append(owned(item, partials[item][0] + arrived.astype(F32)))
                waits = [own[item]]
            else:
                g = item - count
                near = jnp.where(at_end, own[g], halves[item])
                waits, finished = back(g, near, jnp.where(at_end, arrived, middles[item]))


def shards(tokens, routes, gate_probs, gate_up_weight, down_weight, cotangent):
    tok_rows, model_part = tokens.shape
    top_count = routes.shape[1]
    hidden = down_weight.shape[1]
    experts = lax.axis_size("expert")
    capacity = 3 * tok_rows * top_count // (2 * experts)
    half_blocks = experts // HALVES
    half_rows = half_blocks * capacity
    group_tokens = 2 * half_blocks * tok_rows
    group_rows = 2 * half_rows
    mine = lax.axis_index("expert")
    place = lax.axis_index("dp")
    side = (place >= 2).astype(jnp.int32)
    at_end = (place == 0) | (place == lax.axis_size("dp") - 1)

    weight = gate_up_weight.reshape(model_part, 2 * hidden)
    down = down_weight.reshape(hidden, model_part)

    info = jnp.concatenate([routes.astype(F32)] + exact_parts(gate_probs), axis=1)
    info = jnp.pad(info, ((0, 0), (0, LANES - info.shape[1]))).astype(BF16)
    block = jnp.concatenate([tokens, cotangent, info], axis=1)
    near_first = experts == 8
    if near_first:
        blocks = [block, swap(block, 2), swap(block, 4), None]
    else:
        whole = lax.all_gather(block, "expert", axis=0, tiled=True)
        blocks = jnp.split(whole, 4, axis=0)

    lane = lax.broadcasted_iota(jnp.int32, (tok_rows, tok_rows), 1)
    row = lax.broadcasted_iota(jnp.int32, (tok_rows, tok_rows), 0)
    earlier = (lane < row).astype(BF16)
    group_block = jnp.arange(2 * half_blocks, dtype=jnp.int32)
    first_row = ((group_block // half_blocks) ^ side) * half_rows + (group_block % half_blocks) * capacity
    mine_f = mine.astype(F32)

    def front(group):
        named = group[:, 2 * model_part : 2 * model_part + top_count].astype(F32) == mine_f
        named = jnp.any(named, axis=1).reshape(2 * half_blocks, tok_rows)
        before = jnp.dot(named.astype(BF16), earlier.T, preferred_element_type=F32).astype(jnp.int32)
        target = jnp.where(named, before + first_row[:, None], -1).reshape(group_tokens, 1)
        pick = (target == lax.broadcasted_iota(jnp.int32, (group_tokens, group_rows), 1)).astype(BF16)
        picked = lax.dot_general(pick, group, (((0,), (0,)), ((), ())), preferred_element_type=F32).astype(BF16)
        token_rows = picked[:, :model_part]
        grad_rows = picked[:, model_part : 2 * model_part]
        slot_info = picked[:, 2 * model_part :].astype(F32)
        prob = sum(
            slot_info[:, top_count * i : top_count * (i + 1)] for i in (1, 2, 3)
        )
        prob = jnp.sum(jnp.where(slot_info[:, :top_count] == mine_f, prob, 0.0), axis=1, keepdims=True)
        pre = jnp.dot(token_rows, weight, preferred_element_type=F32)
        hidden_grad = lax.dot_general(grad_rows, down, (((1,), (1,)), ((), ())), preferred_element_type=F32)
        partial = jnp.concatenate([pre, hidden_grad], axis=1)
        far = partial[half_rows:].astype(BF16)
        return pick, token_rows, grad_rows, prob, (partial[:half_rows], far, partial[half_rows:]), far

    fronts = []

    def partial_of(g):
        part = blocks[g]
        if near_first:
            if g:
                part = after(part, fronts[g - 1][5])
            part = with_other_core(part)
        fronts.append(front(part))
        if near_first and g == 0:
            blocks[3] = swap(after(block, fronts[0][5]), 6)
        return fronts[g][4]

    def owned(g, total):
        prob = fronts[g][3][:half_rows]
        gate, up, grad = jnp.split(total, 3, axis=1)
        sigmoid_v = jax.nn.sigmoid(gate)
        activated = gate * sigmoid_v
        slopes = sigmoid_v * (1.0 + gate * (1.0 - sigmoid_v))
        act = activated * up
        lanes = lax.broadcasted_iota(jnp.int32, (half_rows, LANES), 1)
        terms = exact_parts(jnp.sum(act * grad, axis=1, keepdims=True))
        extra = sum(jnp.where(lanes == i * experts + mine, terms[i], 0.0) for i in range(3))
        grad = grad * prob
        return jnp.concatenate([act * prob, grad * up * slopes, grad * activated, extra], axis=1).astype(BF16)

    full, wide, sent = {}, {}, {}
    part_rows = group_tokens // 2

    grads = {}

    def gate_up():
        token_rows = jnp.concatenate([f[1] for f in fronts], axis=0)
        grads["rows"] = jnp.concatenate([full[i] for i in range(4)], axis=0)
        grads["gate_up"] = weight_grad(token_rows, (0, model_part), grads["rows"], (hidden, 2 * hidden))
        return grads["gate_up"]

    def back(g, near, far):
        full[g] = jnp.concatenate([near, far], axis=0)
        out = jnp.dot(full[g][:, :hidden], down, preferred_element_type=F32).astype(BF16)
        slot_grad = lax.dot_general(
            full[g][:, hidden : 3 * hidden], weight, (((1,), (1,)), ((), ())), preferred_element_type=F32
        ).astype(BF16)
        row = jnp.concatenate([out, slot_grad, full[g][:, 3 * hidden :]], axis=1)
        wide[g] = jnp.dot(fronts[g][0], row, preferred_element_type=F32).astype(BF16)
        if near_first:
            other = wide[g][part_rows:]
            if g == 3:
                other = after(other, sent[1], sent[2])
            other = swap(other, 1)
            chip_sum = (wide[g][:part_rows].astype(F32) + other.astype(F32)).astype(BF16)
            sent[g] = swap(chip_sum, 2 * g) if g else chip_sum
            return [wide[g]], [chip_sum]
        return [wide[g]], [wide[g]]

    line_pipeline(4, partial_of, owned, at_end, back)
    if near_first:
        summed = sum(sent[g].astype(F32) for g in range(4))
    else:
        whole = jnp.concatenate([wide[g] for g in range(4)], axis=0)
        summed = lax.psum_scatter(whole, "expert", scatter_dimension=0, tiled=True).astype(F32)
    mixed = summed[:, :model_part].astype(BF16)
    token_grad = summed[:, model_part : 2 * model_part].astype(BF16)
    extra = summed[:, 2 * model_part :]
    by_expert = sum(extra[:, i * experts : (i + 1) * experts] for i in range(3))
    chosen = routes[:, :, None] == jnp.arange(experts, dtype=jnp.int32)[None, None, :]
    prob_grad = jnp.sum(jnp.where(chosen, by_expert[:, None, :], 0.0), axis=2)

    gate_up_grad = gate_up()
    grad_rows = jnp.concatenate([f[2] for f in fronts], axis=0)
    down_grad = weight_grad(grads["rows"], (0, hidden), grad_rows, (0, model_part))
    tiles = gate_up_grad.reshape(model_part // 8, 8, 2, hidden).transpose(0, 2, 1, 3)
    tiles = lax.optimization_barrier(tiles)
    return (
        mixed,
        token_grad,
        prob_grad,
        tiles.transpose(0, 2, 1, 3).reshape(1, model_part, 2, hidden),
        down_grad.reshape(1, hidden, model_part),
    )


def solution(mesh):
    placed = (
        P("expert", "dp"),
        P("expert", None),
        P("expert", None),
        P("expert", "dp", None, None),
        P("expert", None, "dp"),
        P("expert", "dp"),
    )
    return jax.shard_map(
        shards,
        mesh=mesh,
        in_specs=placed,
        out_specs=(
            P("expert", "dp"),
            P("expert", "dp"),
            P("expert", None),
            P("expert", "dp", None, None),
            P("expert", None, "dp"),
        ),
        check_vma=False,
    )
```

```python
import functools

import jax
import jax.numpy as jnp
from jax import lax
from jax.experimental import pallas as pl
from jax.experimental.pallas import tpu as pltpu
from jax.sharding import PartitionSpec as P

BF16 = jnp.bfloat16
F32 = jnp.float32
LANES = 128
BLOCK = 256
HALVES = 8


def exact_parts(values):
    first = lax.reduce_precision(values, 8, 7)
    rest = values - first
    second = lax.reduce_precision(rest, 8, 7)
    third = rest - second
    return [first, second, third]


def nothing(*refs):
    pass


def after(array, *results):
    return pl.pallas_call(
        nothing,
        out_shape=jax.ShapeDtypeStruct(array.shape, array.dtype),
        in_specs=[pl.BlockSpec(memory_space=pl.ANY)] * (1 + len(results)),
        out_specs=pl.BlockSpec(memory_space=pl.ANY),
        input_output_aliases={0: 0},
        compiler_params=pltpu.CompilerParams(vmem_limit_bytes=1 << 17),
        name="after",
    )(array, *results)


def grad_block(columns, left_ref, right_ref, out_ref):
    left = left_ref[...]
    out_ref[...] = lax.dot_general(
        left, right_ref[:, columns], (((0,), (0,)), ((), ())), preferred_element_type=F32
    ).astype(BF16)


def weight_grad(left, left_cols, right, right_cols):
    rows = left.shape[0]
    first = left_cols[0] // BLOCK
    wide = right_cols[1]
    return pl.pallas_call(
        functools.partial(grad_block, slice(right_cols[0], right_cols[0] + wide)),
        grid=(left_cols[1] // BLOCK,),
        out_shape=jax.ShapeDtypeStruct((left_cols[1], wide), BF16),
        in_specs=[
            pl.BlockSpec((rows, BLOCK), lambda i: (0, first + i)),
            pl.BlockSpec(right.shape, lambda i: (0, 0), pipeline_mode=pl.Buffered(1)),
        ],
        out_specs=pl.BlockSpec((BLOCK, wide), lambda i: (i, 0)),
        compiler_params=pltpu.CompilerParams(vmem_limit_bytes=14 << 20),
        cost_estimate=pl.CostEstimate(flops=0, bytes_accessed=0, transcendentals=0),
        name="weight_grad",
    )(left, right)


def swap(array, bit):
    size = lax.axis_size("expert")
    return lax.ppermute(array, "expert", [(i, i ^ bit) for i in range(size)])


def with_other_core(part):
    return jnp.concatenate([part, swap(part, 1)], axis=0)


def line_pipeline(count, partial_of, owned, at_end, back):
    last = lax.axis_size("dp") - 1
    inward = [(0, 1), (last, last - 1)]
    middle = [(1, 2), (2, 1)]
    outward = [(1, 0), (2, last)]
    items = 2 * count
    partials = [partial_of(0)]
    own = []
    firsts = [lax.ppermute(partials[0][1], "dp", inward)]
    halves = {}
    second, third, middles, between, across, waits, finished = {}, {}, {}, {}, {}, [], []
    for step in range(items + 2):
        if step < items:
            if step + 1 < count:
                partials.append(partial_of(step + 1))
                sent = partials[step + 1][1]
                waits.append(sent)
            elif step + 1 < items:
                sent = own[step + 1 - count]
            arrived = after(firsts[step], *waits)
            if step + 1 < items:
                firsts.append(lax.ppermute(sent, "dp", inward))
            halves[step] = arrived
            if step < count:
                arrived = (partials[step][2] + arrived.astype(F32)).astype(BF16)
            between[step] = arrived
            second[step] = lax.ppermute(arrived, "dp", middle)
        if 1 <= step <= items:
            item = step - 1
            arrived = second[item]
            if step < items:
                arrived = after(arrived, between[step])
            middles[item] = arrived
            if item < count:
                arrived = (partials[item][0] + arrived.astype(F32)).astype(BF16)
            across[item] = arrived
            third[item] = lax.ppermute(arrived, "dp", outward)
        if step >= 2:
            item = step - 2
            arrived = third[item]
            needs = list(finished) if item > count else []
            if item + 1 < items:
                needs.append(across[item + 1])
            if needs:
                arrived = after(arrived, *needs)
            if item < count:
                own.append(owned(item, partials[item][0] + arrived.astype(F32)))
                waits = [own[item]]
            else:
                g = item - count
                near = jnp.where(at_end, own[g], halves[item])
                waits, finished = back(g, near, jnp.where(at_end, arrived, middles[item]))


def shards(tokens, routes, gate_probs, gate_up_weight, down_weight, cotangent):
    tok_rows, model_part = tokens.shape
    top_count = routes.shape[1]
    hidden = down_weight.shape[1]
    experts = lax.axis_size("expert")
    capacity = 3 * tok_rows * top_count // (2 * experts)
    half_blocks = experts // HALVES
    half_rows = half_blocks * capacity
    group_tokens = 2 * half_blocks * tok_rows
    group_rows = 2 * half_rows
    mine = lax.axis_index("expert")
    place = lax.axis_index("dp")
    side = (place >= 2).astype(jnp.int32)
    at_end = (place == 0) | (place == lax.axis_size("dp") - 1)

    weight = gate_up_weight.reshape(model_part, 2 * hidden)
    down = down_weight.reshape(hidden, model_part)

    info = jnp.concatenate([routes.astype(F32)] + exact_parts(gate_probs), axis=1)
    info = jnp.pad(info, ((0, 0), (0, LANES - info.shape[1]))).astype(BF16)
    block = jnp.concatenate([tokens, cotangent, info], axis=1)
    near_first = experts == 8
    if near_first:
        blocks = [block, swap(block, 2), swap(block, 4), None]
    else:
        whole = lax.all_gather(block, "expert", axis=0, tiled=True)
        blocks = jnp.split(whole, 4, axis=0)

    lane = lax.broadcasted_iota(jnp.int32, (tok_rows, tok_rows), 1)
    row = lax.broadcasted_iota(jnp.int32, (tok_rows, tok_rows), 0)
    earlier = (lane < row).astype(BF16)
    group_block = jnp.arange(2 * half_blocks, dtype=jnp.int32)
    first_row = ((group_block // half_blocks) ^ side) * half_rows + (group_block % half_blocks) * capacity
    mine_f = mine.astype(F32)

    def front(group):
        named = group[:, 2 * model_part : 2 * model_part + top_count].astype(F32) == mine_f
        named = jnp.any(named, axis=1).reshape(2 * half_blocks, tok_rows)
        before = jnp.dot(named.astype(BF16), earlier.T, preferred_element_type=F32).astype(jnp.int32)
        target = jnp.where(named, before + first_row[:, None], -1).reshape(group_tokens, 1)
        pick = (target == lax.broadcasted_iota(jnp.int32, (group_tokens, group_rows), 1)).astype(BF16)
        picked = lax.dot_general(pick, group, (((0,), (0,)), ((), ())), preferred_element_type=F32).astype(BF16)
        token_rows = picked[:, :model_part]
        grad_rows = picked[:, model_part : 2 * model_part]
        slot_info = picked[:, 2 * model_part :].astype(F32)
        prob = sum(
            slot_info[:, top_count * i : top_count * (i + 1)] for i in (1, 2, 3)
        )
        prob = jnp.sum(jnp.where(slot_info[:, :top_count] == mine_f, prob, 0.0), axis=1, keepdims=True)
        pre = jnp.dot(token_rows, weight, preferred_element_type=F32)
        hidden_grad = lax.dot_general(grad_rows, down, (((1,), (1,)), ((), ())), preferred_element_type=F32)
        partial = jnp.concatenate([pre, hidden_grad], axis=1)
        far = partial[half_rows:].astype(BF16)
        return pick, token_rows, grad_rows, prob, (partial[:half_rows], far, partial[half_rows:]), far

    fronts = []

    def partial_of(g):
        part = blocks[g]
        if near_first:
            if g > 1:
                part = after(part, fronts[g - 1][5])
            part = with_other_core(part)
        fronts.append(front(part))
        if near_first and g == 0:
            blocks[3] = swap(after(block, fronts[0][5]), 6)
        return fronts[g][4]

    def owned(g, total):
        prob = fronts[g][3][:half_rows]
        gate, up, grad = jnp.split(total, 3, axis=1)
        sigmoid_v = jax.nn.sigmoid(gate)
        activated = gate * sigmoid_v
        slopes = sigmoid_v * (1.0 + gate * (1.0 - sigmoid_v))
        act = activated * up
        lanes = lax.broadcasted_iota(jnp.int32, (half_rows, LANES), 1)
        terms = exact_parts(jnp.sum(act * grad, axis=1, keepdims=True))
        extra = sum(jnp.where(lanes == i * experts + mine, terms[i], 0.0) for i in range(3))
        grad = grad * prob
        return jnp.concatenate([act * prob, grad * up * slopes, grad * activated, extra], axis=1).astype(BF16)

    full, wide, sent = {}, {}, {}
    part_rows = group_tokens // 2

    grads = {}

    def gate_up():
        token_rows = jnp.concatenate([f[1] for f in fronts], axis=0)
        grads["rows"] = jnp.concatenate([full[i] for i in range(4)], axis=0)
        grads["gate_up"] = weight_grad(token_rows, (0, model_part), grads["rows"], (hidden, 2 * hidden))
        return grads["gate_up"]

    def back(g, near, far):
        full[g] = jnp.concatenate([near, far], axis=0)
        out = jnp.dot(full[g][:, :hidden], down, preferred_element_type=F32).astype(BF16)
        slot_grad = lax.dot_general(
            full[g][:, hidden : 3 * hidden], weight, (((1,), (1,)), ((), ())), preferred_element_type=F32
        ).astype(BF16)
        row = jnp.concatenate([out, slot_grad, full[g][:, 3 * hidden :]], axis=1)
        wide[g] = jnp.dot(fronts[g][0], row, preferred_element_type=F32).astype(BF16)
        if near_first:
            other = wide[g][part_rows:]
            if g == 3:
                other = after(other, sent[1], sent[2])
            other = swap(other, 1)
            chip_sum = (wide[g][:part_rows].astype(F32) + other.astype(F32)).astype(BF16)
            sent[g] = swap(chip_sum, 2 * g) if g else chip_sum
            return [wide[g]], [chip_sum]
        return [wide[g]], [wide[g]]

    line_pipeline(4, partial_of, owned, at_end, back)
    if near_first:
        summed = sum(sent[g].astype(F32) for g in range(4))
    else:
        whole = jnp.concatenate([wide[g] for g in range(4)], axis=0)
        summed = lax.psum_scatter(whole, "expert", scatter_dimension=0, tiled=True).astype(F32)
    mixed = summed[:, :model_part].astype(BF16)
    token_grad = summed[:, model_part : 2 * model_part].astype(BF16)
    extra = summed[:, 2 * model_part :]
    by_expert = sum(extra[:, i * experts : (i + 1) * experts] for i in range(3))
    chosen = routes[:, :, None] == jnp.arange(experts, dtype=jnp.int32)[None, None, :]
    prob_grad = jnp.sum(jnp.where(chosen, by_expert[:, None, :], 0.0), axis=2)

    gate_up_grad = gate_up()
    grad_rows = jnp.concatenate([f[2] for f in fronts], axis=0)
    down_grad = weight_grad(grads["rows"], (0, hidden), grad_rows, (0, model_part))
    tiles = gate_up_grad.reshape(model_part // 8, 8, 2, hidden).transpose(0, 2, 1, 3)
    tiles = lax.optimization_barrier(tiles)
    return (
        mixed,
        token_grad,
        prob_grad,
        tiles.transpose(0, 2, 1, 3).reshape(1, model_part, 2, hidden),
        down_grad.reshape(1, hidden, model_part),
    )


def solution(mesh):
    placed = (
        P("expert", "dp"),
        P("expert", None),
        P("expert", None),
        P("expert", "dp", None, None),
        P("expert", None, "dp"),
        P("expert", "dp"),
    )
    return jax.shard_map(
        shards,
        mesh=mesh,
        in_specs=placed,
        out_specs=(
            P("expert", "dp"),
            P("expert", "dp"),
            P("expert", None),
            P("expert", "dp", None, None),
            P("expert", None, "dp"),
        ),
        check_vma=False,
    )
```
